256 devices in a mesh: ctx: 64 (over y, x, z_hi, core), head: 4 (over z_lo).
Axes of the slice: x: 4, y: 4, z: 8 (z_hi: 2, z_lo: 4; z = z_hi * 4 + z_lo), core: 2. Of those that a mesh axis runs over, the one named last changes fastest.
Arguments:
- query: bfloat16 [16384, 5120], P('ctx', 'head'), may hold values from -113 to 113
- key: bfloat16 [16384, 5120], P('ctx', 'head'), may hold values from -6 to 6
- value: bfloat16 [16384, 5120], P('ctx', 'head'), may hold values from -6 to 6
- blocks: int32 [128, 8], P('ctx'), may hold values from 0 to 127, as said below
- counts: int32 [128], P('ctx'), may hold values from 1 to 8, as said below
- buckets: int32 [128, 8, 128, 128], P('ctx', 'head'), may hold values from 0 to 31
- edge: bfloat16 [128, 8, 128, 128], P('ctx', 'head'), may hold values from 0.3984375 to 2.5
- table: float32 [40, 32], replicated, may hold values from -6 to 6
Outputs:
- attended: bfloat16 [16384, 5120], P('ctx', 'head')
The draws below stay inside these ranges and needn't reach their ends.
Inputs may be any that keep to these rules, and one draw needn't show every extreme that they name: Entry 0 of row g is g itself; the 8 entries of a row are distinct; every entry is a key block on the same context shard of 2 blocks as g or on one of the 3 shards before it, counted cyclically. Only the first counts[g] entries of row g of blocks are live.
All inputs are finite; a program needn't handle non-finite values.
Results may differ from the reference program's by a relative error of at most 0.012.
The reference program's roundings to bfloat16 on the way (of `bias` and `weights`) count: a program that leaves them out, or rounds other values in their place, can miss the bound.
Values may be sent and summed in bfloat16 or wider, within the bound.
A program may use at most 64 MiB of HBM per device.

```python
import math
import jax
import jax.numpy as jnp
from jax import lax

HEADS = 40
HD = 128
BLK = 128
NB = 8
REACH = 4
NBUCKET = 32
TOKENS = 16384
QB_DEV = 2
QBLOCKS = 128


def shared_rows(key):
    return jax.random.truncated_normal(key, -5.0, 5.0, (TOKENS, HEADS * HD), jnp.float32)


def draw_key(key, part):
    base = shared_rows(key)
    return base.astype(jnp.bfloat16)


def draw_query(key, part):
    key = jax.random.fold_in(key, 9)
    fresh = jax.random.truncated_normal(key, -5.0, 5.0, (TOKENS, HEADS * HD), jnp.float32)
    return fresh.astype(jnp.bfloat16)


def draw_blocks(key, part):
    key = jax.random.fold_in(key, 3)
    span = REACH * QB_DEV - 1
    own = jnp.arange(QBLOCKS, dtype=jnp.int32)
    device = own // QB_DEV
    own_pos = (REACH - 1) * QB_DEV + own % QB_DEV
    scores = jax.random.randint(key, (QBLOCKS, span), 0, 1 << 20) * span + jnp.arange(span, dtype=jnp.int32)[None, :]
    picks = jnp.argsort(scores, axis=1)[:, :NB - 1].astype(jnp.int32)
    picks = picks + (picks >= own_pos[:, None]).astype(jnp.int32)
    others = ((device[:, None] - REACH + 1) * QB_DEV + picks) % QBLOCKS
    return jnp.concatenate([own[:, None], others], axis=1).astype(jnp.int32)


def draw_counts(key, part):
    key = jax.random.fold_in(key, 5)
    first, second = jax.random.split(key)
    level = jax.random.randint(first, (QBLOCKS // QB_DEV,), 1, 5)
    spread = jnp.repeat(level, QB_DEV)
    jitter = jax.random.randint(second, (QBLOCKS,), 0, 2)
    result = jnp.clip(spread * NB // 4 - jitter, 1, NB)
    result = result.at[0].set(NB)
    return result.astype(jnp.int32)


def touch_ends(values, key, low, high):
    shape = values.shape
    place = [jax.random.randint(jax.random.fold_in(key, axis), (), 0, shape[axis]) for axis in range(len(shape))]
    values = values.at[tuple(place)].set(low)
    longest = shape.index(max(shape))
    place[longest] = (place[longest] + 1) % shape[longest]
    return values.at[tuple(place)].set(high)


def levels(stream_key, shape, pieces, least, top_value):
    level, own = 1.0, jax.random.fold_in(stream_key, 6)
    for axis_at, parts in pieces:
        steps = jnp.exp(jax.random.uniform(jax.random.fold_in(own, axis_at), (parts,), jnp.float32, least / len(pieces), top_value / len(pieces)))
        level = level * jnp.repeat(steps, shape[axis_at] // parts).reshape([-1 if axis == axis_at else 1 for axis in range(len(shape))])
    return level


def centred(rng, dims, deviation, bound, pieces=(), kind=jnp.bfloat16):
    level = levels(rng, dims, pieces, -0.22, 0.18) if pieces else 1.0
    entries = jax.random.normal(rng, dims, jnp.float32) * deviation * level
    return jnp.minimum(jnp.maximum(entries, -bound), bound).astype(kind)


def setup_inputs(seed: int = 0) -> dict:
    seeds = jax.random.split(jax.random.key(seed), 9)
    query = draw_query(jax.random.fold_in(seeds[8], 71), 0)
    key = draw_key(jax.random.fold_in(seeds[8], 71), 0)
    value = centred(seeds[2], (TOKENS, HEADS * HD), 1.0, 6.0, ((0, 64), (1, 4)))
    blocks = draw_blocks(jax.random.fold_in(seeds[8], 71), 0)
    counts = draw_counts(jax.random.fold_in(seeds[8], 71), 0)
    buckets = touch_ends(jax.random.randint(seeds[5], (QBLOCKS, NB, BLK, BLK), 0, NBUCKET), jax.random.fold_in(seeds[5], 1), 0, NBUCKET - 1).astype(jnp.int32)
    edge = jnp.clip(jnp.exp(math.log(2.5) - 1.8364954 * jax.random.uniform(seeds[6], (QBLOCKS, NB, BLK, BLK), jnp.float32) ** levels(seeds[6], (QBLOCKS, NB, BLK, BLK), ((0, 64), (1, 4)), -0.2, 0.2)), 0.3984375, 2.5).astype(jnp.bfloat16)
    table = centred(seeds[7], (HEADS, NBUCKET), 1.5, 6.0, (), jnp.float32)
    return dict(query=query, key=key, value=value, blocks=blocks, counts=counts, buckets=buckets, edge=edge, table=table)


def reference(query, key, value, blocks, counts, buckets, edge, table):
    scale = HD ** -0.5
    q_all = query.reshape(QBLOCKS, BLK, HEADS, HD)
    k_all = key.reshape(QBLOCKS, BLK, HEADS, HD)
    v_all = value.reshape(QBLOCKS, BLK, HEADS, HD)

    def one_block(g):
        q_rows = q_all[g].astype(jnp.float32)
        listed = blocks[g]
        k_rows = k_all[listed].astype(jnp.float32)
        v_rows = v_all[listed].astype(jnp.float32)
        looked = table[:, buckets[g]] * edge[g].astype(jnp.float32)[None]
        bias = lax.optimization_barrier(looked.astype(jnp.bfloat16)).astype(jnp.float32)
        scores = jnp.einsum("ahd,nbhd->hanb", q_rows, k_rows) * scale + jnp.transpose(bias, (0, 2, 1, 3))
        live = jnp.arange(NB, dtype=jnp.int32) < counts[g]
        scores = jnp.where(live[None, None, :, None], scores, jnp.float32(-1e30))
        high = jnp.max(scores, axis=(2, 3), keepdims=True)
        weights = lax.optimization_barrier(jnp.exp(scores - high).astype(jnp.bfloat16)).astype(jnp.float32)
        total = jnp.sum(weights, axis=(2, 3))
        mixed = jnp.einsum("hanb,nbhd->ahd", weights, v_rows) / jnp.transpose(total)[:, :, None]
        return mixed.astype(jnp.bfloat16).reshape(BLK, HEADS * HD)

    result = lax.map(one_block, jnp.arange(QBLOCKS, dtype=jnp.int32))
    return result.reshape(TOKENS, HEADS * HD)
```

```python
import jax
import jax.numpy as jnp
from jax import lax
from jax.experimental import pallas as pl
from jax.experimental.pallas import tpu as pltpu
from jax.sharding import PartitionSpec as P

HD = 128
BLK = 128
REACH = 4
DEAD = -1e30
MESH = pl.DeviceIdType.MESH


def attention_kernel(
    nctx,
    blocks_ref,
    counts_ref,
    q_hbm,
    k_hbm,
    v_hbm,
    buckets_hbm,
    edge_hbm,
    table_ref,
    out_hbm,
    q_vm,
    kv_own,
    kv_in,
    bucket_raw,
    bucket_all,
    edge_all,
    index_vm,
    edge_vm,
    table_vm,
    scores_vm,
    out_vm,
    local_sem,
    out_sem,
    kv_send,
    kv_recv,
    tile_send,
    tile_recv,
):
    nheads = kv_own.shape[1]
    nlevels = table_ref.shape[1]
    ctx = lax.axis_index("ctx")
    head = lax.axis_index("head")
    core = lax.rem(ctx, 2)
    head_near = head + 1 - 2 * lax.rem(head, 2)
    head_two = lax.rem(head + 2, 4)
    head_far = 3 - head
    middle = jnp.logical_or(head == 1, head == 2)

    def at_ctx(shift):
        return (lax.rem(ctx + shift + nctx, nctx), head)

    next_chip, prev_chip = at_ctx(2), at_ctx(-2)
    third_to, third_from = at_ctx(1 + 2 * core), at_ctx(2 * core - 3)
    partner = at_ctx(1 - 2 * core)

    bucket_load = pltpu.make_async_copy(buckets_hbm, bucket_raw, local_sem.at[0])
    edge_load = pltpu.make_async_copy(edge_hbm, edge_all.at[head], local_sem.at[1])
    q_load = pltpu.make_async_copy(q_hbm, q_vm, local_sem.at[2])
    bucket_load.start()
    edge_load.start()
    q_load.start()

    def own_load(pair, c):
        src = (k_hbm, v_hbm)[pair]
        return pltpu.make_async_copy(
            src.at[:, pl.ds(pl.multiple_of(c * HD, HD), HD)],
            kv_own.at[pair, c],
            local_sem.at[3 + pair * nheads + c],
        )

    def load_own(c, carry):
        own_load(0, c).start()
        own_load(1, c).start()
        return carry

    lax.fori_loop(0, nheads, load_own, 0)

    barrier = pltpu.get_barrier_semaphore()
    peers = [
        next_chip,
        prev_chip,
        third_to,
        third_from,
        (ctx, head_near),
        (ctx, head_two),
        (ctx, head_far),
    ]
    for peer in peers:
        pl.semaphore_signal(barrier, inc=1, device_id=peer, device_id_type=MESH)
    pl.semaphore_wait(barrier, len(peers))

    def kv_copy(flow, pair, c, target):
        if flow == 1:
            src = kv_in.at[0, pair, c]
        else:
            src = (k_hbm, v_hbm)[pair].at[:, pl.ds(pl.multiple_of(c * HD, HD), HD)]
        return pltpu.make_async_remote_copy(
            src_ref=src,
            dst_ref=kv_in.at[flow, pair, c],
            send_sem=kv_send.at[flow, pair, c],
            recv_sem=kv_recv.at[flow, pair, c],
            device_id=target,
            device_id_type=MESH,
        )

    def tile_copy(which, origin, slot, target):
        if which == 0:
            src = bucket_all.at[origin]
            dst = bucket_all.at[origin]
        else:
            src = edge_all.at[origin]
            dst = edge_all.at[origin]
        return pltpu.make_async_remote_copy(
            src_ref=src,
            dst_ref=dst,
            send_sem=tile_send.at[which, slot],
            recv_sem=tile_recv.at[which, origin],
            device_id=(ctx, target),
            device_id_type=MESH,
        )

    bucket_load.wait()
    bucket_all[head] = bucket_raw[...].astype(jnp.float32).astype(jnp.bfloat16)
    edge_load.wait()
    for which in range(2):
        tile_copy(which, head, 1, head_two).start()
        tile_copy(which, head, 0, head_near).start()

    @pl.when(middle)
    def _():
        for which in range(2):
            tile_copy(which, head, 2, head_far).start()

    def send_own(c, carry):
        for pair in range(2):
            kv_copy(0, pair, c, next_chip).start()
        for pair in range(2):
            kv_copy(2, pair, c, third_to).start()
        return carry

    lax.fori_loop(0, nheads, send_own, 0)

    table_vm[...] = jnp.full_like(table_vm, DEAD)
    table_vm[:, 0:nlevels] = table_ref[...]

    for which in range(2):
        tile_copy(which, head_two, 1, head_two).wait_recv()

    @pl.when(middle)
    def _():
        for which in range(2):
            tile_copy(which, head_two, 3, head_near).start()

    for which in range(2):
        tile_copy(which, head_near, 0, head_near).wait_recv()
        tile_copy(which, head_far, 2, head_near).wait_recv()

    behind = (0, 2, 1 + 2 * core, 3 - 2 * core)
    for g in range(2):
        for j in range(REACH):
            home = lax.rem(ctx - behind[j] + nctx, nctx)
            for b in range(2):
                block = home * 2 + b
                entry = jnp.int32(0)
                for n in range(8):
                    entry = jnp.where(blocks_ref[g, n] == block, n, entry)
                dead = entry >= counts_ref[g]
                origin, part = entry // 2, entry % 2
                found = bucket_all[origin, g, part].astype(jnp.float32).astype(jnp.int32)
                index_vm[g, j * 2 + b] = jnp.where(dead, nlevels, found)
                edge_vm[g, j * 2 + b] = edge_all[origin, g, part].astype(jnp.float32)

    q_load.wait()
    scale = HD ** (-0.5)

    def one_head(c, carry):
        for pair in range(2):
            kv_copy(0, pair, c, next_chip).wait_recv()
            kv_copy(1, pair, c, partner).start()
        for pair in range(2):
            own_load(pair, c).wait()
            kv_copy(2, pair, c, third_to).wait_recv()
        for pair in range(2):
            kv_copy(1, pair, c, partner).wait_recv()

        queries = q_vm[:, pl.ds(pl.multiple_of(c * HD, HD), HD)]
        row = table_vm[pl.ds(head * nheads + c, 1), :]
        levels = jnp.broadcast_to(row, (BLK, HD))
        high = [jnp.full((BLK, BLK), -jnp.inf, jnp.float32) for _ in range(2)]
        for j in range(REACH):
            keys = kv_own[0, c] if j == 0 else kv_in[j - 1, 0, c]
            raw = lax.dot_general(
                queries, keys, (((1,), (1,)), ((), ())), preferred_element_type=jnp.float32
            )
            for g in range(2):
                for b in range(2):
                    looked = jnp.take_along_axis(levels, index_vm[g, j * 2 + b], axis=1)
                    bias = (looked * edge_vm[g, j * 2 + b]).astype(jnp.bfloat16)
                    tile = raw[g * BLK : (g + 1) * BLK, b * BLK : (b + 1) * BLK] * scale
                    tile = tile + bias.astype(jnp.float32)
                    high[g] = jnp.maximum(high[g], tile)
                    scores_vm[pl.ds(g * BLK, BLK), pl.ds((j * 2 + b) * BLK, BLK)] = tile
        top = jnp.concatenate([jnp.max(x, axis=1, keepdims=True) for x in high], axis=0)
        mixed = jnp.zeros((2 * BLK, 2 * HD), jnp.float32)
        ones = jnp.ones((2 * BLK, HD), jnp.bfloat16)
        for j in range(REACH):
            vals = kv_own[1, c] if j == 0 else kv_in[j - 1, 1, c]
            weights = jnp.exp(scores_vm[:, pl.ds(j * 2 * BLK, 2 * BLK)] - top)
            mixed = mixed + jnp.dot(
                weights.astype(jnp.bfloat16),
                jnp.concatenate([vals, ones], axis=1),
                preferred_element_type=jnp.float32,
            )
        out_vm[c] = (mixed[:, :HD] / mixed[:, HD:]).astype(jnp.bfloat16)
        out_copy(c).start()
        return carry

    def out_copy(c):
        return pltpu.make_async_copy(
            out_vm.at[c],
            out_hbm.at[:, pl.ds(pl.multiple_of(c * HD, HD), HD)],
            out_sem.at[c],
        )

    lax.fori_loop(0, nheads, one_head, 0)

    def finish(c, carry):
        out_copy(c).wait()
        for pair in range(2):
            kv_copy(0, pair, c, next_chip).wait_send()
            kv_copy(1, pair, c, partner).wait_send()
            kv_copy(2, pair, c, third_to).wait_send()
        return carry

    lax.fori_loop(0, nheads, finish, 0)
    for which in range(2):
        tile_copy(which, head, 1, head_two).wait_send()
        tile_copy(which, head, 0, head_near).wait_send()

    @pl.when(middle)
    def _():
        for which in range(2):
            tile_copy(which, head, 2, head_far).wait_send()
            tile_copy(which, head_two, 3, head_near).wait_send()


def body(query, key, value, blocks, counts, buckets, edge, table):
    rows, width = query.shape
    nheads = width // HD
    nctx = lax.axis_size("ctx")
    anywhere = pl.BlockSpec(memory_space=pl.ANY)
    scalars = pl.BlockSpec(memory_space=pltpu.SMEM)
    tiles = (2, 2, BLK, BLK)

    def kernel(*refs):
        attention_kernel(nctx, *refs)

    return pl.pallas_call(
        kernel,
        out_shape=jax.ShapeDtypeStruct((rows, width), jnp.bfloat16),
        in_specs=[scalars, scalars] + [anywhere] * 5 + [pl.BlockSpec(memory_space=pltpu.VMEM)],
        out_specs=anywhere,
        scratch_shapes=[
            pltpu.VMEM((rows, width), jnp.bfloat16),
            pltpu.VMEM((2, nheads, rows, HD), jnp.bfloat16),
            pltpu.VMEM((3, 2, nheads, rows, HD), jnp.bfloat16),
            pltpu.VMEM(tiles, jnp.int32),
            pltpu.VMEM((4,) + tiles, jnp.bfloat16),
            pltpu.VMEM((4,) + tiles, jnp.bfloat16),
            pltpu.VMEM((2, 8, BLK, BLK), jnp.int32),
            pltpu.VMEM((2, 8, BLK, BLK), jnp.float32),
            pltpu.VMEM((table.shape[0], 128), jnp.float32),
            pltpu.VMEM((rows, 8 * BLK), jnp.float32),
            pltpu.VMEM((nheads, rows, HD), jnp.bfloat16),
            pltpu.SemaphoreType.DMA((3 + 2 * nheads,)),
            pltpu.SemaphoreType.DMA((nheads,)),
            pltpu.SemaphoreType.DMA((3, 2, nheads)),
            pltpu.SemaphoreType.DMA((3, 2, nheads)),
            pltpu.SemaphoreType.DMA((2, 4)),
            pltpu.SemaphoreType.DMA((2, 4)),
        ],
        compiler_params=pltpu.CompilerParams(
            collective_id=0, has_side_effects=True, vmem_limit_bytes=60 * 2**20
        ),
        name="attention",
    )(blocks, counts, query, key, value, buckets, edge, table)


def solution(mesh):
    return jax.shard_map(
        body,
        mesh=mesh,
        in_specs=(
            P("ctx", "head"),
            P("ctx", "head"),
            P("ctx", "head"),
            P("ctx", None),
            P("ctx"),
            P("ctx", "head", None, None),
            P("ctx", "head", None, None),
            P(),
        ),
        out_specs=P("ctx", "head"),
        check_vma=False,
    )
```

```python
import functools

import jax
import jax.numpy as jnp
from jax import lax
from jax.experimental import pallas as pl
from jax.experimental.pallas import tpu as pltpu
from jax.sharding import PartitionSpec as P

HD = 128
BLK = 128
REACH = 4
DEAD = -1e30
PIECE = 2
AHEAD = 2
MESH = pl.DeviceIdType.MESH


def attention_kernel(
    nctx,
    blocks_ref,
    counts_ref,
    q_hbm,
    k_hbm,
    v_hbm,
    buckets_hbm,
    edge_hbm,
    table_hbm,
    out_hbm,
    q_vm,
    kv_own,
    kv_in,
    bucket_raw,
    bucket_all,
    edge_all,
    index_vm,
    edge_vm,
    table_raw,
    table_vm,
    scores_vm,
    out_vm,
    local_sem,
    out_sem,
    kv_send,
    kv_recv,
    tile_send,
    tile_recv,
):
    pieces = kv_own.shape[1]
    nheads = out_vm.shape[0]
    wide = PIECE * HD
    nlevels = table_raw.shape[1]
    ctx = lax.axis_index("ctx")
    head = lax.axis_index("head")
    core = lax.rem(ctx, 2)
    head_near = head + 1 - 2 * lax.rem(head, 2)
    head_two = lax.rem(head + 2, 4)
    head_far = 3 - head
    middle = jnp.logical_or(head == 1, head == 2)

    def at_ctx(shift):
        return (lax.rem(ctx + shift + nctx, nctx), head)

    next_chip, prev_chip = at_ctx(2), at_ctx(-2)
    third_to, third_from = at_ctx(1 + 2 * core), at_ctx(2 * core - 3)
    partner = at_ctx(1 - 2 * core)

    bucket_load = pltpu.make_async_copy(buckets_hbm, bucket_raw, local_sem.at[0])
    edge_load = pltpu.make_async_copy(edge_hbm, edge_all.at[head], local_sem.at[1])
    q_load = pltpu.make_async_copy(q_hbm, q_vm, local_sem.at[2])
    table_load = pltpu.make_async_copy(table_hbm, table_raw, local_sem.at[3])
    bucket_load.start()
    edge_load.start()
    q_load.start()
    table_load.start()

    def own_load(pair, c):
        src = (k_hbm, v_hbm)[pair]
        return pltpu.make_async_copy(
            src.at[:, pl.ds(pl.multiple_of(c * wide, HD), wide)],
            kv_own.at[pair, c],
            local_sem.at[4 + pair * pieces + c],
        )

    def load_own(c, carry):
        own_load(0, c).start()
        own_load(1, c).start()
        return carry

    lax.fori_loop(0, pieces, load_own, 0)

    barrier = pltpu.get_barrier_semaphore()
    peers = [
        next_chip,
        prev_chip,
        third_to,
        third_from,
        (ctx, head_near),
        (ctx, head_two),
        (ctx, head_far),
    ]
    for peer in peers:
        pl.semaphore_signal(barrier, inc=1, device_id=peer, device_id_type=MESH)
    pl.semaphore_wait(barrier, len(peers))

    def kv_copy(flow, pair, c, target):
        if flow == 1:
            src = kv_in.at[0, pair, c]
        else:
            src = (k_hbm, v_hbm)[pair].at[:, pl.ds(pl.multiple_of(c * wide, HD), wide)]
        return pltpu.make_async_remote_copy(
            src_ref=src,
            dst_ref=kv_in.at[flow, pair, c],
            send_sem=kv_send.at[flow, pair, c],
            recv_sem=kv_recv.at[flow, pair, c],
            device_id=target,
            device_id_type=MESH,
        )

    def tile_copy(which, origin, slot, target):
        if which == 0:
            src = bucket_all.at[origin]
            dst = bucket_all.at[origin]
        else:
            src = edge_all.at[origin]
            dst = edge_all.at[origin]
        return pltpu.make_async_remote_copy(
            src_ref=src,
            dst_ref=dst,
            send_sem=tile_send.at[which, slot],
            recv_sem=tile_recv.at[which, origin],
            device_id=(ctx, target),
            device_id_type=MESH,
        )

    bucket_load.wait()
    bucket_all[head] = bucket_raw[...].astype(jnp.float32).astype(jnp.bfloat16)
    edge_load.wait()
    for which in range(2):
        tile_copy(which, head, 1, head_two).start()
        tile_copy(which, head, 0, head_near).start()

    @pl.when(middle)
    def _():
        for which in range(2):
            tile_copy(which, head, 2, head_far).start()

    def send_own(c, carry):
        for pair in range(2):
            kv_copy(0, pair, c, next_chip).start()
        for pair in range(2):
            kv_copy(2, pair, c, third_to).start()
        return carry

    lax.fori_loop(0, AHEAD, send_own, 0)

    table_load.wait()
    table_vm[...] = jnp.full_like(table_vm, DEAD)
    table_vm[:, 0:nlevels] = table_raw[...]

    for which in range(2):
        tile_copy(which, head_two, 1, head_two).wait_recv()

    @pl.when(middle)
    def _():
        for which in range(2):
            tile_copy(which, head_two, 3, head_near).start()

    for which in range(2):
        tile_copy(which, head_near, 0, head_near).wait_recv()
        tile_copy(which, head_far, 2, head_near).wait_recv()

    behind = (0, 2, 1 + 2 * core, 3 - 2 * core)
    for g in range(2):
        for j in range(REACH):
            home = lax.rem(ctx - behind[j] + nctx, nctx)
            for b in range(2):
                block = home * 2 + b
                entry = jnp.int32(0)
                for n in range(8):
                    entry = jnp.where(blocks_ref[g, n] == block, n, entry)
                dead = entry >= counts_ref[g]
                origin, part = entry // 2, entry % 2
                found = bucket_all[origin, g, part].astype(jnp.float32).astype(jnp.int32)
                index_vm[g, j * 2 + b] = jnp.where(dead, nlevels, found)
                edge_vm[g, j * 2 + b] = edge_all[origin, g, part].astype(jnp.float32)

    q_load.wait()
    scale = HD ** (-0.5)

    def one_piece(c, carry):
        for pair in range(2):
            kv_copy(0, pair, c, next_chip).wait_recv()
            kv_copy(1, pair, c, partner).start()

        @pl.when(c + AHEAD < pieces)
        def _():
            send_own(c + AHEAD, 0)

        for pair in range(2):
            own_load(pair, c).wait()
            kv_copy(2, pair, c, third_to).wait_recv()
        for pair in range(2):
            kv_copy(1, pair, c, partner).wait_recv()
        return lax.fori_loop(0, PIECE, functools.partial(one_head, c), carry)

    def one_head(piece, part, carry):
        c = piece * PIECE + part
        columns = pl.ds(pl.multiple_of(part * HD, HD), HD)
        queries = q_vm[:, pl.ds(pl.multiple_of(c * HD, HD), HD)]
        row = table_vm[pl.ds(head * nheads + c, 1), :]
        levels = jnp.broadcast_to(row, (BLK, HD))
        high = [jnp.full((BLK, BLK), -jnp.inf, jnp.float32) for _ in range(2)]
        for j in range(REACH):
            keys = kv_own[0, piece, :, columns] if j == 0 else kv_in[j - 1, 0, piece, :, columns]
            raw = lax.dot_general(
                queries, keys, (((1,), (1,)), ((), ())), preferred_element_type=jnp.float32
            )
            for g in range(2):
                for b in range(2):
                    looked = jnp.take_along_axis(levels, index_vm[g, j * 2 + b], axis=1)
                    bias = (looked * edge_vm[g, j * 2 + b]).astype(jnp.bfloat16)
                    tile = raw[g * BLK : (g + 1) * BLK, b * BLK : (b + 1) * BLK] * scale
                    tile = tile + bias.astype(jnp.float32)
                    high[g] = jnp.maximum(high[g], tile)
                    scores_vm[pl.ds(g * BLK, BLK), pl.ds((j * 2 + b) * BLK, BLK)] = tile
        top = jnp.concatenate([jnp.max(x, axis=1, keepdims=True) for x in high], axis=0)
        mixed = jnp.zeros((2 * BLK, 2 * HD), jnp.float32)
        ones = jnp.ones((2 * BLK, HD), jnp.bfloat16)
        for j in range(REACH):
            vals = kv_own[1, piece, :, columns] if j == 0 else kv_in[j - 1, 1, piece, :, columns]
            weights = jnp.exp(scores_vm[:, pl.ds(j * 2 * BLK, 2 * BLK)] - top)
            mixed = mixed + jnp.dot(
                weights.astype(jnp.bfloat16),
                jnp.concatenate([vals, ones], axis=1),
                preferred_element_type=jnp.float32,
            )
        out_vm[c] = (mixed[:, :HD] / mixed[:, HD:]).astype(jnp.bfloat16)
        out_copy(c).start()
        return carry

    def out_copy(c):
        return pltpu.make_async_copy(
            out_vm.at[c],
            out_hbm.at[:, pl.ds(pl.multiple_of(c * HD, HD), HD)],
            out_sem.at[c],
        )

    lax.fori_loop(0, pieces, one_piece, 0)

    def finish_out(c, carry):
        out_copy(c).wait()
        return carry

    lax.fori_loop(0, nheads, finish_out, 0)

    def finish(c, carry):
        for pair in range(2):
            kv_copy(0, pair, c, next_chip).wait_send()
            kv_copy(1, pair, c, partner).wait_send()
            kv_copy(2, pair, c, third_to).wait_send()
        return carry

    lax.fori_loop(0, pieces, finish, 0)
    for which in range(2):
        tile_copy(which, head, 1, head_two).wait_send()
        tile_copy(which, head, 0, head_near).wait_send()

    @pl.when(middle)
    def _():
        for which in range(2):
            tile_copy(which, head, 2, head_far).wait_send()
            tile_copy(which, head_two, 3, head_near).wait_send()


def body(query, key, value, blocks, counts, buckets, edge, table):
    rows, width = query.shape
    nheads = width // HD
    pieces = nheads // PIECE
    nctx = lax.axis_size("ctx")
    anywhere = pl.BlockSpec(memory_space=pl.ANY)
    scalars = pl.BlockSpec(memory_space=pltpu.SMEM)
    tiles = (2, 2, BLK, BLK)

    def kernel(*refs):
        attention_kernel(nctx, *refs)

    return pl.pallas_call(
        kernel,
        out_shape=jax.ShapeDtypeStruct((rows, width), jnp.bfloat16),
        in_specs=[scalars, scalars] + [anywhere] * 6,
        out_specs=anywhere,
        scratch_shapes=[
            pltpu.VMEM((rows, width), jnp.bfloat16),
            pltpu.VMEM((2, pieces, rows, PIECE * HD), jnp.bfloat16),
            pltpu.VMEM((3, 2, pieces, rows, PIECE * HD), jnp.bfloat16),
            pltpu.VMEM(tiles, jnp.int32),
            pltpu.VMEM((4,) + tiles, jnp.bfloat16),
            pltpu.VMEM((4,) + tiles, jnp.bfloat16),
            pltpu.VMEM((2, 8, BLK, BLK), jnp.int32),
            pltpu.VMEM((2, 8, BLK, BLK), jnp.float32),
            pltpu.VMEM(table.shape, jnp.float32),
            pltpu.VMEM((table.shape[0], 128), jnp.float32),
            pltpu.VMEM((rows, 8 * BLK), jnp.float32),
            pltpu.VMEM((nheads, rows, HD), jnp.bfloat16),
            pltpu.SemaphoreType.DMA((4 + 2 * pieces,)),
            pltpu.SemaphoreType.DMA((nheads,)),
            pltpu.SemaphoreType.DMA((3, 2, pieces)),
            pltpu.SemaphoreType.DMA((3, 2, pieces)),
            pltpu.SemaphoreType.DMA((2, 4)),
            pltpu.SemaphoreType.DMA((2, 4)),
        ],
        compiler_params=pltpu.CompilerParams(
            collective_id=0, has_side_effects=True, vmem_limit_bytes=60 * 2**20
        ),
        name="attention",
    )(blocks, counts, query, key, value, buckets, edge, table)


def solution(mesh):
    return jax.shard_map(
        body,
        mesh=mesh,
        in_specs=(
            P("ctx", "head"),
            P("ctx", "head"),
            P("ctx", "head"),
            P("ctx", None),
            P("ctx"),
            P("ctx", "head", None, None),
            P("ctx", "head", None, None),
            P(),
        ),
        out_specs=P("ctx", "head"),
        check_vma=False,
    )
```

```python
import jax
import jax.numpy as jnp
from jax import lax
from jax.experimental import pallas as pl
from jax.experimental.pallas import tpu as pltpu
from jax.sharding import PartitionSpec as P

HD = 128
BLK = 128
REACH = 4
DEAD = -1e30
AHEAD = 4
MESH = pl.DeviceIdType.MESH


def attention_kernel(
    nctx,
    blocks_ref,
    counts_ref,
    q_hbm,
    k_hbm,
    v_hbm,
    buckets_hbm,
    edge_hbm,
    table_hbm,
    out_ref,
    q_vm,
    kv_own,
    kv_in,
    bucket_raw,
    bucket_all,
    edge_all,
    index_vm,
    edge_vm,
    table_raw,
    table_vm,
    scores_vm,
    local_sem,
    kv_send,
    kv_recv,
    tile_send,
    tile_recv,
):
    nheads = kv_own.shape[1]
    nlevels = table_raw.shape[0]
    ctx = lax.axis_index("ctx")
    head = lax.axis_index("head")
    core = lax.rem(ctx, 2)
    head_near = head + 1 - 2 * lax.rem(head, 2)
    head_two = lax.rem(head + 2, 4)
    head_far = 3 - head
    middle = jnp.logical_or(head == 1, head == 2)

    def at_ctx(shift):
        return (lax.rem(ctx + shift + nctx, nctx), head)

    next_chip, prev_chip = at_ctx(2), at_ctx(-2)
    third_to, third_from = at_ctx(1 + 2 * core), at_ctx(2 * core - 3)
    partner = at_ctx(1 - 2 * core)

    bucket_load = pltpu.make_async_copy(buckets_hbm, bucket_raw, local_sem.at[0])
    edge_load = pltpu.make_async_copy(edge_hbm, edge_all.at[head], local_sem.at[1])
    q_load = pltpu.make_async_copy(q_hbm, q_vm, local_sem.at[2])
    table_load = pltpu.make_async_copy(table_hbm, table_raw, local_sem.at[3])
    bucket_load.start()
    edge_load.start()
    q_load.start()
    table_load.start()

    def own_load(pair, c):
        src = (k_hbm, v_hbm)[pair]
        return pltpu.make_async_copy(
            src.at[:, pl.ds(pl.multiple_of(c * HD, HD), HD)],
            kv_own.at[pair, c],
            local_sem.at[4 + pair * nheads + c],
        )

    def load_own(c, carry):
        own_load(0, c).start()
        own_load(1, c).start()
        return carry

    lax.fori_loop(0, nheads, load_own, 0)

    barrier = pltpu.get_barrier_semaphore()
    peers = [
        next_chip,
        prev_chip,
        third_to,
        third_from,
        (ctx, head_near),
        (ctx, head_two),
        (ctx, head_far),
    ]
    for peer in peers:
        pl.semaphore_signal(barrier, inc=1, device_id=peer, device_id_type=MESH)
    pl.semaphore_wait(barrier, len(peers))

    def kv_copy(flow, pair, c, target):
        if flow == 1:
            src = kv_in.at[0, pair, c]
        else:
            src = (k_hbm, v_hbm)[pair].at[:, pl.ds(pl.multiple_of(c * HD, HD), HD)]
        return pltpu.make_async_remote_copy(
            src_ref=src,
            dst_ref=kv_in.at[flow, pair, c],
            send_sem=kv_send.at[flow, pair, c],
            recv_sem=kv_recv.at[flow, pair, c],
            device_id=target,
            device_id_type=MESH,
        )

    def tile_copy(which, origin, slot, target):
        if which == 0:
            src = bucket_all.at[origin]
            dst = bucket_all.at[origin]
        else:
            src = edge_all.at[origin]
            dst = edge_all.at[origin]
        return pltpu.make_async_remote_copy(
            src_ref=src,
            dst_ref=dst,
            send_sem=tile_send.at[which, slot],
            recv_sem=tile_recv.at[which, origin],
            device_id=(ctx, target),
            device_id_type=MESH,
        )

    bucket_load.wait()
    bucket_all[head] = bucket_raw[...].astype(jnp.float32).astype(jnp.bfloat16)
    edge_load.wait()
    for which in range(2):
        tile_copy(which, head, 1, head_two).start()
        tile_copy(which, head, 0, head_near).start()

    @pl.when(middle)
    def _():
        for which in range(2):
            tile_copy(which, head, 2, head_far).start()

    def send_own(c, carry):
        for pair in range(2):
            kv_copy(0, pair, c, next_chip).start()
        for pair in range(2):
            kv_copy(2, pair, c, third_to).start()
        return carry

    lax.fori_loop(0, AHEAD, send_own, 0)

    table_load.wait()
    table_vm[...] = jnp.full_like(table_vm, DEAD)
    table_vm[0:nlevels, 0 : table_raw.shape[1]] = table_raw[...]
    table_vm[...] = table_vm[...].T

    for which in range(2):
        tile_copy(which, head_two, 1, head_two).wait_recv()

    @pl.when(middle)
    def _():
        for which in range(2):
            tile_copy(which, head_two, 3, head_near).start()

    for which in range(2):
        tile_copy(which, head_near, 0, head_near).wait_recv()
        tile_copy(which, head_far, 2, head_near).wait_recv()

    behind = (0, 2, 1 + 2 * core, 3 - 2 * core)
    for g in range(2):
        for j in range(REACH):
            home = lax.rem(ctx - behind[j] + nctx, nctx)
            for b in range(2):
                block = home * 2 + b
                entry = jnp.int32(0)
                for n in range(8):
                    entry = jnp.where(blocks_ref[g, n] == block, n, entry)
                dead = entry >= counts_ref[g]
                origin, part = entry // 2, entry % 2
                found = bucket_all[origin, g, part].astype(jnp.float32).astype(jnp.int32)
                index_vm[g, j * 2 + b] = jnp.where(dead, nlevels, found)
                edge_vm[g, j * 2 + b] = edge_all[origin, g, part].astype(jnp.float32)

    q_load.wait()
    scale = HD ** (-0.5)

    def arrive(c):
        for pair in range(2):
            kv_copy(0, pair, c, next_chip).wait_recv()
            kv_copy(1, pair, c, partner).start()

    def attend(c):
        for pair in range(2):
            own_load(pair, c).wait()
            kv_copy(2, pair, c, third_to).wait_recv()
            kv_copy(1, pair, c, partner).wait_recv()
        columns = pl.ds(pl.multiple_of(c * HD, HD), HD)
        queries = q_vm[:, columns]
        row = table_vm[pl.ds(head * nheads + c, 1), :]
        levels = jnp.broadcast_to(row, (BLK, HD))
        high = [jnp.full((BLK, BLK), -jnp.inf, jnp.float32) for _ in range(2)]
        for j in range(REACH):
            keys = kv_own[0, c] if j == 0 else kv_in[j - 1, 0, c]
            raw = lax.dot_general(
                queries, keys, (((1,), (1,)), ((), ())), preferred_element_type=jnp.float32
            )
            for g in range(2):
                for b in range(2):
                    looked = jnp.take_along_axis(levels, index_vm[g, j * 2 + b], axis=1)
                    bias = (looked * edge_vm[g, j * 2 + b]).astype(jnp.bfloat16)
                    tile = raw[g * BLK : (g + 1) * BLK, b * BLK : (b + 1) * BLK] * scale
                    tile = tile + bias.astype(jnp.float32)
                    high[g] = jnp.maximum(high[g], tile)
                    scores_vm[pl.ds(g * BLK, BLK), pl.ds((j * 2 + b) * BLK, BLK)] = tile
        top = jnp.concatenate([jnp.max(x, axis=1, keepdims=True) for x in high], axis=0)
        mixed = jnp.zeros((2 * BLK, 2 * HD), jnp.float32)
        ones = jnp.ones((2 * BLK, HD), jnp.bfloat16)
        for j in range(REACH):
            vals = kv_own[1, c] if j == 0 else kv_in[j - 1, 1, c]
            weights = jnp.exp(scores_vm[:, pl.ds(j * 2 * BLK, 2 * BLK)] - top)
            mixed = mixed + jnp.dot(
                weights.astype(jnp.bfloat16),
                jnp.concatenate([vals, ones], axis=1),
                preferred_element_type=jnp.float32,
            )
        out_ref[:, columns] = (mixed[:, :HD] / mixed[:, HD:]).astype(jnp.bfloat16)

    def one_head(c, carry):
        @pl.when(c < nheads)
        def _():
            arrive(c)

        @pl.when(c + AHEAD < nheads)
        def _():
            send_own(c + AHEAD, 0)

        @pl.when(c > 0)
        def _():
            attend(c - 1)

        return carry

    lax.fori_loop(0, nheads + 1, one_head, 0)

    def finish(c, carry):
        for pair in range(2):
            kv_copy(0, pair, c, next_chip).wait_send()
            kv_copy(1, pair, c, partner).wait_send()
            kv_copy(2, pair, c, third_to).wait_send()
        return carry

    lax.fori_loop(0, nheads, finish, 0)
    for which in range(2):
        tile_copy(which, head, 1, head_two).wait_send()
        tile_copy(which, head, 0, head_near).wait_send()

    @pl.when(middle)
    def _():
        for which in range(2):
            tile_copy(which, head, 2, head_far).wait_send()
            tile_copy(which, head_two, 3, head_near).wait_send()


def body(query, key, value, blocks, counts, buckets, edge, table):
    rows, width = query.shape
    nheads = width // HD
    nctx = lax.axis_size("ctx")
    anywhere = pl.BlockSpec(memory_space=pl.ANY)
    scalars = pl.BlockSpec(memory_space=pltpu.SMEM)
    tiles = (2, 2, BLK, BLK)

    def kernel(*refs):
        attention_kernel(nctx, *refs)

    return pl.pallas_call(
        kernel,
        out_shape=pltpu.VMEM((rows, width), jnp.bfloat16),
        in_specs=[scalars, scalars] + [anywhere] * 6,
        out_specs=pl.BlockSpec(memory_space=pltpu.VMEM),
        scratch_shapes=[
            pltpu.VMEM((rows, width), jnp.bfloat16),
            pltpu.VMEM((2, nheads, rows, HD), jnp.bfloat16),
            pltpu.VMEM((3, 2, nheads, rows, HD), jnp.bfloat16),
            pltpu.VMEM(tiles, jnp.int32),
            pltpu.VMEM((4,) + tiles, jnp.bfloat16),
            pltpu.VMEM((4,) + tiles, jnp.bfloat16),
            pltpu.VMEM((2, 8, BLK, BLK), jnp.int32),
            pltpu.VMEM((2, 8, BLK, BLK), jnp.float32),
            pltpu.VMEM(table.shape[::-1], jnp.float32),
            pltpu.VMEM((128, 128), jnp.float32),
            pltpu.VMEM((rows, 8 * BLK), jnp.float32),
            pltpu.SemaphoreType.DMA((4 + 2 * nheads,)),
            pltpu.SemaphoreType.DMA((3, 2, nheads)),
            pltpu.SemaphoreType.DMA((3, 2, nheads)),
            pltpu.SemaphoreType.DMA((2, 4)),
            pltpu.SemaphoreType.DMA((2, 4)),
        ],
        compiler_params=pltpu.CompilerParams(
            collective_id=0, has_side_effects=True, vmem_limit_bytes=60 * 2**20
        ),
        name="attention",
    )(blocks, counts, query, key, value, buckets, edge, table.T)


def solution(mesh):
    return jax.shard_map(
        body,
        mesh=mesh,
        in_specs=(
            P("ctx", "head"),
            P("ctx", "head"),
            P("ctx", "head"),
            P("ctx", None),
            P("ctx"),
            P("ctx", "head", None, None),
            P("ctx", "head", None, None),
            P(),
        ),
        out_specs=P("ctx", "head"),
        check_vma=False,
    )
```

```python
import jax
import jax.numpy as jnp
from jax import lax
from jax.experimental import pallas as pl
from jax.experimental.pallas import tpu as pltpu
from jax.sharding import PartitionSpec as P

HD = 128
BLK = 128
REACH = 4
DEAD = -1e30
AHEAD = 4
LATE = 5
TURNED = (9,)
RELAY_AT = 3
MESH = pl.DeviceIdType.MESH


def attention_kernel(
    nctx,
    blocks_ref,
    counts_ref,
    q_hbm,
    k_hbm,
    v_hbm,
    buckets_hbm,
    edge_hbm,
    table_hbm,
    out_ref,
    q_vm,
    kv_own,
    kv_in,
    bucket_raw,
    bucket_all,
    edge_all,
    index_vm,
    edge_vm,
    table_raw,
    table_vm,
    scores_vm,
    local_sem,
    kv_send,
    kv_recv,
    tile_send,
    tile_recv,
    turn_in,
    turn_send,
    turn_recv,
):
    nheads = kv_own.shape[1]
    nlevels = table_raw.shape[0]
    ctx = lax.axis_index("ctx")
    head = lax.axis_index("head")
    core = lax.rem(ctx, 2)
    head_near = head + 1 - 2 * lax.rem(head, 2)
    head_two = lax.rem(head + 2, 4)
    head_far = 3 - head
    middle = jnp.logical_or(head == 1, head == 2)
    upper = lax.rem(ctx, 4) // 2 == 1
    turns = jnp.logical_and(jnp.logical_not(middle), upper)
    relays = jnp.logical_and(jnp.logical_not(middle), jnp.logical_not(upper))

    def at_ctx(shift):
        return (lax.rem(ctx + shift + nctx, nctx), head)

    next_chip, prev_chip = at_ctx(2), at_ctx(-2)
    third_to, third_from = at_ctx(1 + 2 * core), at_ctx(2 * core - 3)
    partner = at_ctx(1 - 2 * core)

    barrier = pltpu.get_barrier_semaphore()
    peers = [
        prev_chip,
        third_from,
        partner,
        (ctx, head_near),
        (ctx, head_two),
        (ctx, head_far),
    ]
    for peer in peers:
        pl.semaphore_signal(barrier, inc=1, device_id=peer, device_id_type=MESH)

    @pl.when(relays)
    def _():
        pl.semaphore_signal(
            barrier, inc=1, device_id=(prev_chip[0], head_far), device_id_type=MESH
        )

    bucket_load = pltpu.make_async_copy(buckets_hbm, bucket_raw, local_sem.at[0])
    edge_load = pltpu.make_async_copy(edge_hbm, edge_all.at[head], local_sem.at[1])
    q_load = pltpu.make_async_copy(q_hbm, q_vm, local_sem.at[2])
    table_load = pltpu.make_async_copy(table_hbm, table_raw, local_sem.at[3])
    bucket_load.start()
    edge_load.start()
    q_load.start()
    table_load.start()

    def own_load(pair, c):
        src = (k_hbm, v_hbm)[pair]
        return pltpu.make_async_copy(
            src.at[:, pl.ds(pl.multiple_of(c * HD, HD), HD)],
            kv_own.at[pair, c],
            local_sem.at[4 + pair * nheads + c],
        )

    def load_own(c, carry):
        own_load(0, c).start()
        own_load(1, c).start()
        return carry

    def kv_copy(flow, pair, c, target):
        if flow == 1:
            src = kv_in.at[0, pair, c]
        else:
            src = (k_hbm, v_hbm)[pair].at[:, pl.ds(pl.multiple_of(c * HD, HD), HD)]
        return pltpu.make_async_remote_copy(
            src_ref=src,
            dst_ref=kv_in.at[flow, pair, c],
            send_sem=kv_send.at[flow, pair, c],
            recv_sem=kv_recv.at[flow, pair, c],
            device_id=target,
            device_id_type=MESH,
        )

    def tile_copy(which, origin, slot, target):
        if which == 0:
            src = bucket_all.at[origin]
            dst = bucket_all.at[origin]
        else:
            src = edge_all.at[origin]
            dst = edge_all.at[origin]
        return pltpu.make_async_remote_copy(
            src_ref=src,
            dst_ref=dst,
            send_sem=tile_send.at[which, slot],
            recv_sem=tile_recv.at[which, origin],
            device_id=(ctx, target),
            device_id_type=MESH,
        )

    bucket_load.wait()
    bucket_all[head] = bucket_raw[...].astype(jnp.float32).astype(jnp.bfloat16)
    edge_load.wait()
    pl.semaphore_wait(barrier, len(peers) + jnp.where(turns, 1, 0))
    for which in range(2):
        tile_copy(which, head, 1, head_two).start()
        tile_copy(which, head, 0, head_near).start()

    @pl.when(middle)
    def _():
        for which in range(2):
            tile_copy(which, head, 2, head_far).start()

    def turn_copy(pair, t):
        return pltpu.make_async_remote_copy(
            src_ref=(k_hbm, v_hbm)[pair].at[:, pl.ds(TURNED[t] * HD, HD)],
            dst_ref=turn_in.at[pair, t],
            send_sem=kv_send.at[0, pair, TURNED[t]],
            recv_sem=turn_recv.at[pair, t],
            device_id=(next_chip[0], head_far),
            device_id_type=MESH,
        )

    def relay_copy(pair, t):
        return pltpu.make_async_remote_copy(
            src_ref=turn_in.at[pair, t],
            dst_ref=kv_in.at[0, pair, TURNED[t]],
            send_sem=turn_send.at[pair, t],
            recv_sem=kv_recv.at[0, pair, TURNED[t]],
            device_id=(ctx, head_far),
            device_id_type=MESH,
        )

    def send_own(c, carry):
        turned = c < 0
        for piece in TURNED:
            turned = jnp.logical_or(turned, c == piece)
        turned = jnp.logical_and(turned, turns)

        @pl.when(jnp.logical_not(turned))
        def _():
            for pair in range(2):
                kv_copy(0, pair, c, next_chip).start()

        for pair in range(2):
            kv_copy(2, pair, c, third_to).start()
        return carry

    lax.fori_loop(0, 2, send_own, 0)

    @pl.when(turns)
    def _():
        for t in range(len(TURNED)):
            for pair in range(2):
                turn_copy(pair, t).start()

    lax.fori_loop(0, nheads, load_own, 0)

    table_load.wait()
    table_vm[...] = jnp.full_like(table_vm, DEAD)
    table_vm[0:nlevels, 0 : table_raw.shape[1]] = table_raw[...]
    table_vm[...] = table_vm[...].T

    for which in range(2):
        tile_copy(which, head_two, 1, head_two).wait_recv()

    @pl.when(middle)
    def _():
        for which in range(2):
            tile_copy(which, head_two, 3, head_near).start()

    for which in range(2):
        tile_copy(which, head_near, 0, head_near).wait_recv()
        tile_copy(which, head_far, 2, head_near).wait_recv()

    lax.fori_loop(2, AHEAD, send_own, 0)

    behind = (0, 2, 1 + 2 * core, 3 - 2 * core)
    for g in range(2):
        for j in range(REACH):
            home = lax.rem(ctx - behind[j] + nctx, nctx)
            for b in range(2):
                block = home * 2 + b
                entry = jnp.int32(0)
                for n in range(8):
                    entry = jnp.where(blocks_ref[g, n] == block, n, entry)
                dead = entry >= counts_ref[g]
                origin, part = entry // 2, entry % 2
                found = bucket_all[origin, g, part].astype(jnp.float32).astype(jnp.int32)
                index_vm[g, j * 2 + b] = jnp.where(dead, nlevels, found)
                edge_vm[g, j * 2 + b] = edge_all[origin, g, part].astype(jnp.float32)

    q_load.wait()
    scale = HD ** (-0.5)

    def arrive(c):
        for pair in range(2):
            kv_copy(0, pair, c, next_chip).wait_recv()
            kv_copy(1, pair, c, partner).start()

    def attend(c):
        for pair in range(2):
            own_load(pair, c).wait()
            kv_copy(2, pair, c, third_to).wait_recv()
            kv_copy(1, pair, c, partner).wait_recv()
        columns = pl.ds(pl.multiple_of(c * HD, HD), HD)
        queries = q_vm[:, columns]
        row = table_vm[pl.ds(head * nheads + c, 1), :]
        levels = jnp.broadcast_to(row, (BLK, HD))
        high = [jnp.full((BLK, BLK), -jnp.inf, jnp.float32) for _ in range(2)]
        for j in range(REACH):
            keys = kv_own[0, c] if j == 0 else kv_in[j - 1, 0, c]
            raw = lax.dot_general(
                queries, keys, (((1,), (1,)), ((), ())), preferred_element_type=jnp.float32
            )
            for g in range(2):
                for b in range(2):
                    looked = jnp.take_along_axis(levels, index_vm[g, j * 2 + b], axis=1)
                    bias = (looked * edge_vm[g, j * 2 + b]).astype(jnp.bfloat16)
                    tile = raw[g * BLK : (g + 1) * BLK, b * BLK : (b + 1) * BLK] * scale
                    tile = tile + bias.astype(jnp.float32)
                    high[g] = jnp.maximum(high[g], tile)
                    scores_vm[pl.ds(g * BLK, BLK), pl.ds((j * 2 + b) * BLK, BLK)] = tile
        top = jnp.concatenate([jnp.max(x, axis=1, keepdims=True) for x in high], axis=0)
        mixed = jnp.zeros((2 * BLK, 2 * HD), jnp.float32)
        ones = jnp.ones((2 * BLK, HD), jnp.bfloat16)
        for j in range(REACH):
            vals = kv_own[1, c] if j == 0 else kv_in[j - 1, 1, c]
            weights = jnp.exp(scores_vm[:, pl.ds(j * 2 * BLK, 2 * BLK)] - top)
            mixed = mixed + jnp.dot(
                weights.astype(jnp.bfloat16),
                jnp.concatenate([vals, ones], axis=1),
                preferred_element_type=jnp.float32,
            )
        out_ref[:, columns] = (mixed[:, :HD] / mixed[:, HD:]).astype(jnp.bfloat16)

    def sent(c):
        for pair in range(2):
            kv_copy(0, pair, c, next_chip).wait_send()
            kv_copy(1, pair, c, partner).wait_send()
            kv_copy(2, pair, c, third_to).wait_send()

    def one_head(c, carry):
        for t in range(len(TURNED)):

            @pl.when(jnp.logical_and(relays, c == RELAY_AT + t))
            def _():
                for pair in range(2):
                    turn_copy(pair, t).wait_recv()
                    relay_copy(pair, t).start()

        @pl.when(c < nheads)
        def _():
            arrive(c)

        @pl.when(c + AHEAD < nheads)
        def _():
            send_own(c + AHEAD, 0)

        @pl.when(c > 0)
        def _():
            attend(c - 1)

        @pl.when(c >= LATE)
        def _():
            sent(c - LATE)

        return carry

    lax.fori_loop(0, nheads + 1, one_head, 0)

    def finish(c, carry):
        sent(c)
        return carry

    lax.fori_loop(nheads + 1 - LATE, nheads, finish, 0)
    @pl.when(relays)
    def _():
        for t in range(len(TURNED)):
            for pair in range(2):
                relay_copy(pair, t).wait_send()

    for which in range(2):
        tile_copy(which, head, 1, head_two).wait_send()
        tile_copy(which, head, 0, head_near).wait_send()

    @pl.when(middle)
    def _():
        for which in range(2):
            tile_copy(which, head, 2, head_far).wait_send()
            tile_copy(which, head_two, 3, head_near).wait_send()


def body(query, key, value, blocks, counts, buckets, edge, table):
    rows, width = query.shape
    nheads = width // HD
    nctx = lax.axis_size("ctx")
    anywhere = pl.BlockSpec(memory_space=pl.ANY)
    scalars = pl.BlockSpec(memory_space=pltpu.SMEM)
    tiles = (2, 2, BLK, BLK)

    def kernel(*refs):
        attention_kernel(nctx, *refs)

    return pl.pallas_call(
        kernel,
        out_shape=pltpu.VMEM((rows, width), jnp.bfloat16),
        in_specs=[scalars, scalars] + [anywhere] * 6,
        out_specs=pl.BlockSpec(memory_space=pltpu.VMEM),
        scratch_shapes=[
            pltpu.VMEM((rows, width), jnp.bfloat16),
            pltpu.VMEM((2, nheads, rows, HD), jnp.bfloat16),
            pltpu.VMEM((3, 2, nheads, rows, HD), jnp.bfloat16),
            pltpu.VMEM(tiles, jnp.int32),
            pltpu.VMEM((4,) + tiles, jnp.bfloat16),
            pltpu.VMEM((4,) + tiles, jnp.bfloat16),
            pltpu.VMEM((2, 8, BLK, BLK), jnp.int32),
            pltpu.VMEM((2, 8, BLK, BLK), jnp.float32),
            pltpu.VMEM(table.shape[::-1], jnp.float32),
            pltpu.VMEM((128, 128), jnp.float32),
            pltpu.VMEM((rows, 8 * BLK), jnp.float32),
            pltpu.SemaphoreType.DMA((4 + 2 * nheads,)),
            pltpu.SemaphoreType.DMA((3, 2, nheads)),
            pltpu.SemaphoreType.DMA((3, 2, nheads)),
            pltpu.SemaphoreType.DMA((2, 4)),
            pltpu.SemaphoreType.DMA((2, 4)),
            pltpu.VMEM((2, len(TURNED), rows, HD), jnp.bfloat16),
            pltpu.SemaphoreType.DMA((2, len(TURNED))),
            pltpu.SemaphoreType.DMA((2, len(TURNED))),
        ],
        compiler_params=pltpu.CompilerParams(
            collective_id=0, has_side_effects=True, vmem_limit_bytes=60 * 2**20
        ),
        name="attention",
    )(blocks, counts, query, key, value, buckets, edge, table.T)


def solution(mesh):
    return jax.shard_map(
        body,
        mesh=mesh,
        in_specs=(
            P("ctx", "head"),
            P("ctx", "head"),
            P("ctx", "head"),
            P("ctx", None),
            P("ctx"),
            P("ctx", "head", None, None),
            P("ctx", "head", None, None),
            P(),
        ),
        out_specs=P("ctx", "head"),
        check_vma=False,
    )
```

```python
import jax
import jax.numpy as jnp
from jax import lax
from jax.experimental import pallas as pl
from jax.experimental.pallas import tpu as pltpu
from jax.sharding import PartitionSpec as P

HD = 128
BLK = 128
REACH = 4
DEAD = -1e30
AHEAD = 4
LATE = 5
TURNED = (9,)
RELAY_AT = 3
MESH = pl.DeviceIdType.MESH


def attention_kernel(
    nctx,
    blocks_ref,
    counts_ref,
    q_hbm,
    k_hbm,
    v_hbm,
    buckets_hbm,
    edge_hbm,
    table_hbm,
    out_ref,
    q_vm,
    kv_own,
    kv_in,
    bucket_raw,
    bucket_all,
    edge_all,
    index_vm,
    edge_vm,
    table_raw,
    table_vm,
    scores_vm,
    high_vm,
    local_sem,
    kv_send,
    kv_recv,
    tile_send,
    tile_recv,
    turn_in,
    turn_send,
    turn_recv,
):
    nheads = kv_own.shape[1]
    nlevels = table_raw.shape[0]
    ctx = lax.axis_index("ctx")
    head = lax.axis_index("head")
    core = lax.rem(ctx, 2)
    head_near = head + 1 - 2 * lax.rem(head, 2)
    head_two = lax.rem(head + 2, 4)
    head_far = 3 - head
    middle = jnp.logical_or(head == 1, head == 2)
    upper = lax.rem(ctx, 4) // 2 == 1
    turns = jnp.logical_and(jnp.logical_not(middle), upper)
    relays = jnp.logical_and(jnp.logical_not(middle), jnp.logical_not(upper))

    def at_ctx(shift):
        return (lax.rem(ctx + shift + nctx, nctx), head)

    next_chip, prev_chip = at_ctx(2), at_ctx(-2)
    third_to, third_from = at_ctx(1 + 2 * core), at_ctx(2 * core - 3)
    partner = at_ctx(1 - 2 * core)

    barrier = pltpu.get_barrier_semaphore()
    peers = [
        prev_chip,
        third_from,
        partner,
        (ctx, head_near),
        (ctx, head_two),
        (ctx, head_far),
    ]
    for peer in peers:
        pl.semaphore_signal(barrier, inc=1, device_id=peer, device_id_type=MESH)

    @pl.when(relays)
    def _():
        pl.semaphore_signal(
            barrier, inc=1, device_id=(prev_chip[0], head_far), device_id_type=MESH
        )

    bucket_load = pltpu.make_async_copy(buckets_hbm, bucket_raw, local_sem.at[0])
    edge_load = pltpu.make_async_copy(edge_hbm, edge_all.at[head], local_sem.at[1])
    q_load = pltpu.make_async_copy(q_hbm, q_vm, local_sem.at[2])
    table_load = pltpu.make_async_copy(table_hbm, table_raw, local_sem.at[3])
    bucket_load.start()
    edge_load.start()
    q_load.start()
    table_load.start()

    def own_load(pair, c):
        src = (k_hbm, v_hbm)[pair]
        return pltpu.make_async_copy(
            src.at[:, pl.ds(pl.multiple_of(c * HD, HD), HD)],
            kv_own.at[pair, c],
            local_sem.at[4 + pair * nheads + c],
        )

    def load_own(c, carry):
        own_load(0, c).start()
        own_load(1, c).start()
        return carry

    def kv_copy(flow, pair, c, target):
        if flow == 1:
            src = kv_in.at[0, pair, c]
        else:
            src = (k_hbm, v_hbm)[pair].at[:, pl.ds(pl.multiple_of(c * HD, HD), HD)]
        return pltpu.make_async_remote_copy(
            src_ref=src,
            dst_ref=kv_in.at[flow, pair, c],
            send_sem=kv_send.at[flow, pair, c],
            recv_sem=kv_recv.at[flow, pair, c],
            device_id=target,
            device_id_type=MESH,
        )

    def tile_copy(which, origin, slot, target):
        if which == 0:
            src = bucket_all.at[origin]
            dst = bucket_all.at[origin]
        else:
            src = edge_all.at[origin]
            dst = edge_all.at[origin]
        return pltpu.make_async_remote_copy(
            src_ref=src,
            dst_ref=dst,
            send_sem=tile_send.at[which, slot],
            recv_sem=tile_recv.at[which, origin],
            device_id=(ctx, target),
            device_id_type=MESH,
        )

    bucket_load.wait()
    bucket_all[head] = bucket_raw[...].astype(jnp.float32).astype(jnp.bfloat16)
    edge_load.wait()
    pl.semaphore_wait(barrier, len(peers) + jnp.where(turns, 1, 0))
    for which in range(2):
        tile_copy(which, head, 1, head_two).start()
        tile_copy(which, head, 0, head_near).start()

    @pl.when(middle)
    def _():
        for which in range(2):
            tile_copy(which, head, 2, head_far).start()

    def turn_copy(pair, t):
        return pltpu.make_async_remote_copy(
            src_ref=(k_hbm, v_hbm)[pair].at[:, pl.ds(TURNED[t] * HD, HD)],
            dst_ref=turn_in.at[pair, t],
            send_sem=kv_send.at[0, pair, TURNED[t]],
            recv_sem=turn_recv.at[pair, t],
            device_id=(next_chip[0], head_far),
            device_id_type=MESH,
        )

    def relay_copy(pair, t):
        return pltpu.make_async_remote_copy(
            src_ref=turn_in.at[pair, t],
            dst_ref=kv_in.at[0, pair, TURNED[t]],
            send_sem=turn_send.at[pair, t],
            recv_sem=kv_recv.at[0, pair, TURNED[t]],
            device_id=(ctx, head_far),
            device_id_type=MESH,
        )

    def send_own(c, carry):
        turned = c < 0
        for piece in TURNED:
            turned = jnp.logical_or(turned, c == piece)
        turned = jnp.logical_and(turned, turns)

        @pl.when(jnp.logical_not(turned))
        def _():
            for pair in range(2):
                kv_copy(0, pair, c, next_chip).start()

        for pair in range(2):
            kv_copy(2, pair, c, third_to).start()
        return carry

    lax.fori_loop(0, 2, send_own, 0)

    @pl.when(turns)
    def _():
        for t in range(len(TURNED)):
            for pair in range(2):
                turn_copy(pair, t).start()

    lax.fori_loop(0, nheads, load_own, 0)

    table_load.wait()
    table_vm[...] = jnp.full_like(table_vm, DEAD)
    table_vm[0:nlevels, 0 : table_raw.shape[1]] = table_raw[...]
    table_vm[...] = table_vm[...].T

    for which in range(2):
        tile_copy(which, head_two, 1, head_two).wait_recv()

    @pl.when(middle)
    def _():
        for which in range(2):
            tile_copy(which, head_two, 3, head_near).start()

    for which in range(2):
        tile_copy(which, head_near, 0, head_near).wait_recv()
        tile_copy(which, head_far, 2, head_near).wait_recv()

    lax.fori_loop(2, AHEAD, send_own, 0)

    behind = (0, 2, 1 + 2 * core, 3 - 2 * core)
    for g in range(2):
        for j in range(REACH):
            home = lax.rem(ctx - behind[j] + nctx, nctx)
            for b in range(2):
                block = home * 2 + b
                entry = jnp.int32(0)
                for n in range(8):
                    entry = jnp.where(blocks_ref[g, n] == block, n, entry)
                dead = entry >= counts_ref[g]
                origin, part = entry // 2, entry % 2
                found = bucket_all[origin, g, part].astype(jnp.float32).astype(jnp.int32)
                index_vm[g, j * 2 + b] = jnp.where(dead, nlevels, found)
                edge_vm[g, j * 2 + b] = edge_all[origin, g, part].astype(jnp.float32)

    q_load.wait()
    scale = HD ** (-0.5)

    def arrive(c):
        for pair in range(2):
            kv_copy(0, pair, c, next_chip).wait_recv()
            kv_copy(1, pair, c, partner).start()

    def score(c, j, high):
        columns = pl.ds(pl.multiple_of(c * HD, HD), HD)
        keys = kv_own[0, c] if j == 0 else kv_in[j - 1, 0, c]
        levels = jnp.broadcast_to(table_vm[pl.ds(head * nheads + c, 1), :], (BLK, HD))
        raw = lax.dot_general(
            q_vm[:, columns], keys, (((1,), (1,)), ((), ())), preferred_element_type=jnp.float32
        )
        for g in range(2):
            for b in range(2):
                looked = jnp.take_along_axis(levels, index_vm[g, j * 2 + b], axis=1)
                bias = (looked * edge_vm[g, j * 2 + b]).astype(jnp.bfloat16)
                tile = raw[g * BLK : (g + 1) * BLK, b * BLK : (b + 1) * BLK] * scale
                tile = tile + bias.astype(jnp.float32)
                high[g] = tile if high[g] is None else jnp.maximum(high[g], tile)
                scores_vm[pl.ds(g * BLK, BLK), pl.ds((j * 2 + b) * BLK, BLK)] = tile

    def early(c):
        own_load(0, c).wait()
        high = [None, None]
        score(c, 0, high)
        score(c, 1, high)
        kv_copy(2, 0, c, third_to).wait_recv()
        score(c, 3, high)
        for g in range(2):
            high_vm[g] = high[g]

    def late(c):
        columns = pl.ds(pl.multiple_of(c * HD, HD), HD)
        high = [high_vm[0], high_vm[1]]
        kv_copy(1, 0, c, partner).wait_recv()
        score(c, 2, high)
        top = jnp.concatenate([jnp.max(x, axis=1, keepdims=True) for x in high], axis=0)
        own_load(1, c).wait()
        kv_copy(2, 1, c, third_to).wait_recv()
        kv_copy(1, 1, c, partner).wait_recv()
        mixed = jnp.zeros((2 * BLK, 2 * HD), jnp.float32)
        ones = jnp.ones((2 * BLK, HD), jnp.bfloat16)
        for j in range(REACH):
            vals = kv_own[1, c] if j == 0 else kv_in[j - 1, 1, c]
            weights = jnp.exp(scores_vm[:, pl.ds(j * 2 * BLK, 2 * BLK)] - top)
            mixed = mixed + jnp.dot(
                weights.astype(jnp.bfloat16),
                jnp.concatenate([vals, ones], axis=1),
                preferred_element_type=jnp.float32,
            )
        out_ref[:, columns] = (mixed[:, :HD] / mixed[:, HD:]).astype(jnp.bfloat16)

    def sent(c):
        for pair in range(2):
            kv_copy(0, pair, c, next_chip).wait_send()
            kv_copy(1, pair, c, partner).wait_send()
            kv_copy(2, pair, c, third_to).wait_send()

    def sent_tiles():
        @pl.when(relays)
        def _():
            for t in range(len(TURNED)):
                for pair in range(2):
                    relay_copy(pair, t).wait_send()

        for which in range(2):
            tile_copy(which, head, 1, head_two).wait_send()
            tile_copy(which, head, 0, head_near).wait_send()

        @pl.when(middle)
        def _():
            for which in range(2):
                tile_copy(which, head, 2, head_far).wait_send()
                tile_copy(which, head_two, 3, head_near).wait_send()

    def one_head(c, carry):
        for t in range(len(TURNED)):

            @pl.when(jnp.logical_and(relays, c == RELAY_AT + t))
            def _():
                for pair in range(2):
                    turn_copy(pair, t).wait_recv()
                    relay_copy(pair, t).start()

        @pl.when(c < nheads)
        def _():
            arrive(c)

        @pl.when(c + AHEAD < nheads)
        def _():
            send_own(c + AHEAD, 0)

        @pl.when(c > 0)
        def _():
            late(c - 1)

        @pl.when(c < nheads)
        def _():
            early(c)

        @pl.when(c >= LATE)
        def _():
            sent(c - LATE)

        pl.when(c == nheads - 2)(sent_tiles)

        return carry

    lax.fori_loop(0, nheads + 1, one_head, 0)

    def finish(c, carry):
        sent(c)
        return carry

    lax.fori_loop(nheads + 1 - LATE, nheads, finish, 0)


def body(query, key, value, blocks, counts, buckets, edge, table):
    rows, width = query.shape
    nheads = width // HD
    nctx = lax.axis_size("ctx")
    anywhere = pl.BlockSpec(memory_space=pl.ANY)
    scalars = pl.BlockSpec(memory_space=pltpu.SMEM)
    tiles = (2, 2, BLK, BLK)

    def kernel(*refs):
        attention_kernel(nctx, *refs)

    return pl.pallas_call(
        kernel,
        out_shape=pltpu.VMEM((rows, width), jnp.bfloat16),
        in_specs=[scalars, scalars] + [anywhere] * 6,
        out_specs=pl.BlockSpec(memory_space=pltpu.VMEM),
        scratch_shapes=[
            pltpu.VMEM((rows, width), jnp.bfloat16),
            pltpu.VMEM((2, nheads, rows, HD), jnp.bfloat16),
            pltpu.VMEM((3, 2, nheads, rows, HD), jnp.bfloat16),
            pltpu.VMEM(tiles, jnp.int32),
            pltpu.VMEM((4,) + tiles, jnp.bfloat16),
            pltpu.VMEM((4,) + tiles, jnp.bfloat16),
            pltpu.VMEM((2, 8, BLK, BLK), jnp.int32),
            pltpu.VMEM((2, 8, BLK, BLK), jnp.float32),
            pltpu.VMEM(table.shape[::-1], jnp.float32),
            pltpu.VMEM((128, 128), jnp.float32),
            pltpu.VMEM((rows, 8 * BLK), jnp.float32),
            pltpu.VMEM((2, BLK, BLK), jnp.float32),
            pltpu.SemaphoreType.DMA((4 + 2 * nheads,)),
            pltpu.SemaphoreType.DMA((3, 2, nheads)),
            pltpu.SemaphoreType.DMA((3, 2, nheads)),
            pltpu.SemaphoreType.DMA((2, 4)),
            pltpu.SemaphoreType.DMA((2, 4)),
            pltpu.VMEM((2, len(TURNED), rows, HD), jnp.bfloat16),
            pltpu.SemaphoreType.DMA((2, len(TURNED))),
            pltpu.SemaphoreType.DMA((2, len(TURNED))),
        ],
        compiler_params=pltpu.CompilerParams(
            collective_id=0, has_side_effects=True, vmem_limit_bytes=60 * 2**20
        ),
        name="attention",
    )(blocks, counts, query, key, value, buckets, edge, table.T)


def solution(mesh):
    return jax.shard_map(
        body,
        mesh=mesh,
        in_specs=(
            P("ctx", "head"),
            P("ctx", "head"),
            P("ctx", "head"),
            P("ctx", None),
            P("ctx"),
            P("ctx", "head", None, None),
            P("ctx", "head", None, None),
            P(),
        ),
        out_specs=P("ctx", "head"),
        check_vma=False,
    )
```

```python
import jax
import jax.numpy as jnp
from jax import lax
from jax.experimental import pallas as pl
from jax.experimental.pallas import tpu as pltpu
from jax.sharding import PartitionSpec as P

HD = 128
BLK = 128
REACH = 4
DEAD = -1e30
LATE = 5
TURNED = (9,)
RELAY_AT = 1
MESH = pl.DeviceIdType.MESH


def attention_kernel(
    nctx,
    blocks_ref,
    counts_ref,
    q_hbm,
    k_hbm,
    v_hbm,
    buckets_hbm,
    edge_hbm,
    table_hbm,
    out_ref,
    q_vm,
    kv_own,
    kv_in,
    bucket_raw,
    bucket_all,
    edge_all,
    index_vm,
    edge_vm,
    table_raw,
    table_vm,
    scores_vm,
    high_vm,
    local_sem,
    kv_send,
    kv_recv,
    tile_send,
    tile_recv,
    turn_in,
    turn_send,
    turn_recv,
):
    nheads = kv_own.shape[1]
    nlevels = table_raw.shape[0]
    ctx = lax.axis_index("ctx")
    head = lax.axis_index("head")
    core = lax.rem(ctx, 2)
    head_near = head + 1 - 2 * lax.rem(head, 2)
    head_two = lax.rem(head + 2, 4)
    head_far = 3 - head
    middle = jnp.logical_or(head == 1, head == 2)
    outer = jnp.logical_not(middle)
    upper = lax.rem(ctx, 4) // 2 == 1
    turns = jnp.logical_and(outer, upper)
    relays = jnp.logical_and(outer, jnp.logical_not(upper))

    def at_ctx(shift):
        return (lax.rem(ctx + shift + nctx, nctx), head)

    next_chip, prev_chip = at_ctx(2), at_ctx(-2)
    third_to, third_from = at_ctx(1 + 2 * core), at_ctx(2 * core - 3)
    partner = at_ctx(1 - 2 * core)

    barrier = pltpu.get_barrier_semaphore()
    peers = [
        prev_chip,
        third_from,
        partner,
        (ctx, head_near),
        (ctx, head_two),
        (ctx, head_far),
    ]
    for peer in peers:
        pl.semaphore_signal(barrier, inc=1, device_id=peer, device_id_type=MESH)

    @pl.when(relays)
    def _():
        pl.semaphore_signal(
            barrier, inc=1, device_id=(prev_chip[0], head_far), device_id_type=MESH
        )

    bucket_load = pltpu.make_async_copy(buckets_hbm, bucket_raw, local_sem.at[0])
    edge_load = pltpu.make_async_copy(edge_hbm, edge_all.at[head], local_sem.at[1])
    q_load = pltpu.make_async_copy(q_hbm, q_vm, local_sem.at[2])
    table_load = pltpu.make_async_copy(table_hbm, table_raw, local_sem.at[3])
    bucket_load.start()
    edge_load.start()
    q_load.start()
    table_load.start()

    def own_load(pair, c):
        src = (k_hbm, v_hbm)[pair]
        return pltpu.make_async_copy(
            src.at[:, pl.ds(pl.multiple_of(c * HD, HD), HD)],
            kv_own.at[pair, c],
            local_sem.at[4 + pair * nheads + c],
        )

    def load_own(c, carry):
        own_load(0, c).start()
        own_load(1, c).start()
        return carry

    def kv_copy(flow, pair, c, target):
        if flow == 1:
            src = kv_in.at[0, pair, c]
        else:
            src = (k_hbm, v_hbm)[pair].at[:, pl.ds(pl.multiple_of(c * HD, HD), HD)]
        return pltpu.make_async_remote_copy(
            src_ref=src,
            dst_ref=kv_in.at[flow, pair, c],
            send_sem=kv_send.at[flow, pair, c],
            recv_sem=kv_recv.at[flow, pair, c],
            device_id=target,
            device_id_type=MESH,
        )

    def tile_copy(which, origin, slot, target):
        if which == 0:
            src = bucket_all.at[origin]
            dst = bucket_all.at[origin]
        else:
            src = edge_all.at[origin]
            dst = edge_all.at[origin]
        return pltpu.make_async_remote_copy(
            src_ref=src,
            dst_ref=dst,
            send_sem=tile_send.at[which, slot],
            recv_sem=tile_recv.at[which, origin],
            device_id=(ctx, target),
            device_id_type=MESH,
        )

    bucket_load.wait()
    bucket_all[head] = bucket_raw[...].astype(jnp.float32).astype(jnp.bfloat16)
    edge_load.wait()
    pl.semaphore_wait(barrier, len(peers) + jnp.where(turns, 1, 0))
    @pl.when(outer)
    def _():
        for which in range(2):
            tile_copy(which, head, 1, head_two).start()

    @pl.when(middle)
    def _():
        for which in range(2):
            tile_copy(which, head, 2, head_far).start()

    for which in range(2):
        tile_copy(which, head, 0, head_near).start()

    def turn_copy(pair, t):
        return pltpu.make_async_remote_copy(
            src_ref=(k_hbm, v_hbm)[pair].at[:, pl.ds(TURNED[t] * HD, HD)],
            dst_ref=turn_in.at[pair, t],
            send_sem=kv_send.at[0, pair, TURNED[t]],
            recv_sem=turn_recv.at[pair, t],
            device_id=(next_chip[0], head_far),
            device_id_type=MESH,
        )

    def relay_copy(pair, t):
        return pltpu.make_async_remote_copy(
            src_ref=turn_in.at[pair, t],
            dst_ref=kv_in.at[0, pair, TURNED[t]],
            send_sem=turn_send.at[pair, t],
            recv_sem=kv_recv.at[0, pair, TURNED[t]],
            device_id=(ctx, head_far),
            device_id_type=MESH,
        )

    def send_own(c, carry):
        turned = c < 0
        for piece in TURNED:
            turned = jnp.logical_or(turned, c == piece)
        turned = jnp.logical_and(turned, turns)

        @pl.when(jnp.logical_not(turned))
        def _():
            for pair in range(2):
                kv_copy(0, pair, c, next_chip).start()

        for pair in range(2):
            kv_copy(2, pair, c, third_to).start()
        return carry

    early_sent = jnp.where(middle, 1, 4)
    ahead = jnp.where(middle, 4, 6)
    lax.fori_loop(0, early_sent, send_own, 0)

    @pl.when(turns)
    def _():
        for t in range(len(TURNED)):
            for pair in range(2):
                turn_copy(pair, t).start()

    lax.fori_loop(0, nheads, load_own, 0)

    table_load.wait()
    table_vm[...] = jnp.full_like(table_vm, DEAD)
    table_vm[0:nlevels, 0 : table_raw.shape[1]] = table_raw[...]
    table_vm[...] = table_vm[...].T

    for which in range(2):
        tile_copy(which, head_two, 3, head_near).wait_recv()

        @pl.when(middle)
        def _():
            tile_copy(which, head_two, 3, head_near).start()

    for which in range(2):
        tile_copy(which, head_far, 1, head_near).wait_recv()

        @pl.when(middle)
        def _():
            tile_copy(which, head_far, 1, head_near).start()

    for which in range(2):
        tile_copy(which, head_near, 0, head_near).wait_recv()

    lax.fori_loop(early_sent, ahead, send_own, 0)

    behind = (0, 2, 1 + 2 * core, 3 - 2 * core)
    for g in range(2):
        for j in range(REACH):
            home = lax.rem(ctx - behind[j] + nctx, nctx)
            for b in range(2):
                block = home * 2 + b
                entry = jnp.int32(0)
                for n in range(8):
                    entry = jnp.where(blocks_ref[g, n] == block, n, entry)
                dead = entry >= counts_ref[g]
                origin, part = entry // 2, entry % 2
                found = bucket_all[origin, g, part].astype(jnp.float32).astype(jnp.int32)
                index_vm[g, j * 2 + b] = jnp.where(dead, nlevels, found)
                edge_vm[g, j * 2 + b] = edge_all[origin, g, part].astype(jnp.float32)

    q_load.wait()
    scale = HD ** (-0.5)

    def arrive(c):
        for pair in range(2):
            kv_copy(0, pair, c, next_chip).wait_recv()
            kv_copy(1, pair, c, partner).start()

    def score(c, j, high):
        columns = pl.ds(pl.multiple_of(c * HD, HD), HD)
        keys = kv_own[0, c] if j == 0 else kv_in[j - 1, 0, c]
        levels = jnp.broadcast_to(table_vm[pl.ds(head * nheads + c, 1), :], (BLK, HD))
        raw = lax.dot_general(
            q_vm[:, columns], keys, (((1,), (1,)), ((), ())), preferred_element_type=jnp.float32
        )
        for g in range(2):
            for b in range(2):
                looked = jnp.take_along_axis(levels, index_vm[g, j * 2 + b], axis=1)
                bias = (looked * edge_vm[g, j * 2 + b]).astype(jnp.bfloat16)
                tile = raw[g * BLK : (g + 1) * BLK, b * BLK : (b + 1) * BLK] * scale
                tile = tile + bias.astype(jnp.float32)
                high[g] = tile if high[g] is None else jnp.maximum(high[g], tile)
                scores_vm[pl.ds(g * BLK, BLK), pl.ds((j * 2 + b) * BLK, BLK)] = tile

    def early(c):
        own_load(0, c).wait()
        high = [None, None]
        score(c, 0, high)
        score(c, 1, high)
        kv_copy(2, 0, c, third_to).wait_recv()
        score(c, 3, high)
        for g in range(2):
            high_vm[g] = high[g]

    def late(c):
        columns = pl.ds(pl.multiple_of(c * HD, HD), HD)
        high = [high_vm[0], high_vm[1]]
        kv_copy(1, 0, c, partner).wait_recv()
        score(c, 2, high)
        top = jnp.concatenate([jnp.max(x, axis=1, keepdims=True) for x in high], axis=0)
        own_load(1, c).wait()
        kv_copy(2, 1, c, third_to).wait_recv()
        kv_copy(1, 1, c, partner).wait_recv()
        mixed = jnp.zeros((2 * BLK, 2 * HD), jnp.float32)
        ones = jnp.ones((2 * BLK, HD), jnp.bfloat16)
        for j in range(REACH):
            vals = kv_own[1, c] if j == 0 else kv_in[j - 1, 1, c]
            weights = jnp.exp(scores_vm[:, pl.ds(j * 2 * BLK, 2 * BLK)] - top)
            mixed = mixed + jnp.dot(
                weights.astype(jnp.bfloat16),
                jnp.concatenate([vals, ones], axis=1),
                preferred_element_type=jnp.float32,
            )
        out_ref[:, columns] = (mixed[:, :HD] / mixed[:, HD:]).astype(jnp.bfloat16)

    def sent(c):
        for pair in range(2):
            kv_copy(0, pair, c, next_chip).wait_send()
            kv_copy(1, pair, c, partner).wait_send()
            kv_copy(2, pair, c, third_to).wait_send()

    def sent_tiles():
        @pl.when(relays)
        def _():
            for t in range(len(TURNED)):
                for pair in range(2):
                    relay_copy(pair, t).wait_send()

        for which in range(2):
            tile_copy(which, head, 0, head_near).wait_send()

        @pl.when(outer)
        def _():
            for which in range(2):
                tile_copy(which, head, 1, head_two).wait_send()

        @pl.when(middle)
        def _():
            for which in range(2):
                tile_copy(which, head, 2, head_far).wait_send()
                tile_copy(which, head_far, 1, head_near).wait_send()
                tile_copy(which, head_two, 3, head_near).wait_send()

    def one_head(c, carry):
        for t in range(len(TURNED)):

            @pl.when(jnp.logical_and(relays, c == RELAY_AT + t))
            def _():
                for pair in range(2):
                    turn_copy(pair, t).wait_recv()
                    relay_copy(pair, t).start()

        @pl.when(c < nheads)
        def _():
            arrive(c)

        @pl.when(c + ahead < nheads)
        def _():
            send_own(c + ahead, 0)

        @pl.when(c > 0)
        def _():
            late(c - 1)

        @pl.when(c < nheads)
        def _():
            early(c)

        @pl.when(c >= LATE)
        def _():
            sent(c - LATE)

        pl.when(c == nheads - 2)(sent_tiles)

        return carry

    lax.fori_loop(0, nheads + 1, one_head, 0)

    def finish(c, carry):
        sent(c)
        return carry

    lax.fori_loop(nheads + 1 - LATE, nheads, finish, 0)


def body(query, key, value, blocks, counts, buckets, edge, table):
    rows, width = query.shape
    nheads = width // HD
    nctx = lax.axis_size("ctx")
    anywhere = pl.BlockSpec(memory_space=pl.ANY)
    scalars = pl.BlockSpec(memory_space=pltpu.SMEM)
    tiles = (2, 2, BLK, BLK)

    def kernel(*refs):
        attention_kernel(nctx, *refs)

    return pl.pallas_call(
        kernel,
        out_shape=pltpu.VMEM((rows, width), jnp.bfloat16),
        in_specs=[scalars, scalars] + [anywhere] * 6,
        out_specs=pl.BlockSpec(memory_space=pltpu.VMEM),
        scratch_shapes=[
            pltpu.VMEM((rows, width), jnp.bfloat16),
            pltpu.VMEM((2, nheads, rows, HD), jnp.bfloat16),
            pltpu.VMEM((3, 2, nheads, rows, HD), jnp.bfloat16),
            pltpu.VMEM(tiles, jnp.int32),
            pltpu.VMEM((4,) + tiles, jnp.bfloat16),
            pltpu.VMEM((4,) + tiles, jnp.bfloat16),
            pltpu.VMEM((2, 8, BLK, BLK), jnp.int32),
            pltpu.VMEM((2, 8, BLK, BLK), jnp.float32),
            pltpu.VMEM(table.shape[::-1], jnp.float32),
            pltpu.VMEM((128, 128), jnp.float32),
            pltpu.VMEM((rows, 8 * BLK), jnp.float32),
            pltpu.VMEM((2, BLK, BLK), jnp.float32),
            pltpu.SemaphoreType.DMA((4 + 2 * nheads,)),
            pltpu.SemaphoreType.DMA((3, 2, nheads)),
            pltpu.SemaphoreType.DMA((3, 2, nheads)),
            pltpu.SemaphoreType.DMA((2, 4)),
            pltpu.SemaphoreType.DMA((2, 4)),
            pltpu.VMEM((2, len(TURNED), rows, HD), jnp.bfloat16),
            pltpu.SemaphoreType.DMA((2, len(TURNED))),
            pltpu.SemaphoreType.DMA((2, len(TURNED))),
        ],
        compiler_params=pltpu.CompilerParams(
            collective_id=0, has_side_effects=True, vmem_limit_bytes=60 * 2**20
        ),
        name="attention",
    )(blocks, counts, query, key, value, buckets, edge, table.T)


def solution(mesh):
    return jax.shard_map(
        body,
        mesh=mesh,
        in_specs=(
            P("ctx", "head"),
            P("ctx", "head"),
            P("ctx", "head"),
            P("ctx", None),
            P("ctx"),
            P("ctx", "head", None, None),
            P("ctx", "head", None, None),
            P(),
        ),
        out_specs=P("ctx", "head"),
        check_vma=False,
    )
```
